256 devices in a mesh: rep: 16 (over z_hi, x, core), fsdp: 16 (over z_lo, y).
Axes of the slice: x: 4, y: 4, z: 8 (z_hi: 2, z_lo: 4; z = z_hi * 4 + z_lo), core: 2. Of those that a mesh axis runs over, the one named last changes fastest.
Arguments:
- hidden: bfloat16 [16, 7168, 2048], P('rep', 'fsdp'), may hold values from -6 to 6
- target: bfloat16 [16, 2048, 2048], P('rep', 'fsdp'), may hold values from -6 to 6
- weights: bfloat16 [16, 7168, 2048], P('rep', 'fsdp'), may hold values from -0.0625 to 0.0625
- moment: bfloat16 [16, 7168, 2048], P('rep', 'fsdp'), may hold values from -0.75 to 0.75
- second: bfloat16 [16, 7168, 2048], P('rep', 'fsdp'), may hold values from 0.0024871826 to 0.25
- round_index: int32 [1], replicated, may hold values from 0 to 999
Outputs:
- averaged: bfloat16 [16, 7168, 2048], P('rep', 'fsdp')
- new_moment: bfloat16 [16, 7168, 2048], P('rep', 'fsdp')
- hidden_grad: bfloat16 [16, 7168, 2048], P('rep', 'fsdp')
The draws below stay inside these ranges and needn't reach their ends.
Inputs may be any that keep to these rules, and one draw needn't show every extreme that they name: The partner group lies 2 ** (round_index modulo 3) groups away in the XOR sense.
All inputs are finite; a program needn't handle non-finite values.
Results may differ from the reference program's by a relative error of at most 0.02.
Values may be sent and summed in bfloat16 or wider, within the bound.
A program may use at most 128 MiB of HBM per device.

```python
import math
import jax
import jax.numpy as jnp
from jax import lax

D = 2048
FW = 7168
GROUP_TOKENS = 2048
FW_DEV = 448
LEVELS = 3
N_REP = 16


def levels(key, dims, shards, low, top_value):
    def one(position, parts):
        heights = jax.random.uniform(jax.random.fold_in(jax.random.fold_in(key, 6), position), (parts,), jnp.float32, low / len(shards), top_value / len(shards))
        return jnp.repeat(jnp.exp(heights), dims[position] // parts).reshape((-1,) + (1,) * (len(dims) - position - 1))

    factor_of = one(*shards[0])
    for cut in shards[1:]:
        factor_of = factor_of * one(*cut)
    return factor_of


def gaussian(stream_key, extent, spread, limit, shards=(), kind=jnp.bfloat16):
    gain = levels(stream_key, extent, shards, -0.22, 0.18) if shards else 1.0
    result = jax.random.normal(stream_key, extent, jnp.float32) * spread * gain
    return jnp.minimum(jnp.maximum(result, -limit), limit).astype(kind)


def setup_inputs(seed: int = 0) -> dict:
    key_of = jax.random.split(jax.random.key(seed), 7)
    return {
        "hidden": gaussian(key_of[0], (N_REP, FW, GROUP_TOKENS), 1.0, 6.0, ((0, 16), (1, 16))),
        "target": gaussian(key_of[1], (N_REP, GROUP_TOKENS, D), 1.0, 6.0, ((0, 16), (1, 16))),
        "weights": gaussian(key_of[2], (N_REP, FW, D), FW ** -0.5, 0.0625, ((0, 16), (1, 16))),
        "moment": gaussian(key_of[3], (N_REP, FW, D), 0.05, 0.75, ((0, 16), (1, 16))),
        "second": jnp.clip(jnp.exp(math.log(0.25) - 4.61031033 * jax.random.uniform(key_of[4], (N_REP, FW, D), jnp.float32) ** levels(key_of[4], (N_REP, FW, D), ((0, 16), (1, 16)), -0.2, 0.2)), 0.0024871826, 0.25).astype(jnp.bfloat16),
        "round_index": jax.random.randint(key_of[5], (1,), 0, 1000).astype(jnp.int32),
    }


corr_first = 0.9999734386011124
corr_second = 0.994079470779666

def add_block(total, pair):
    hidden_block, weight_block = pair
    term = lax.dot_general(hidden_block, weight_block, (((0,), (0,)), ((), ())), preferred_element_type=jnp.float32)
    rounded = lax.optimization_barrier(term.astype(jnp.bfloat16))
    return (total + rounded.astype(jnp.float32), None)

def one_group(items):
    hidden_cols, target_rows, weight_now, moment_now, second_now = items
    blocks_hidden = hidden_cols.reshape(FW // FW_DEV, FW_DEV, GROUP_TOKENS)
    blocks_weight = weight_now.reshape(FW // FW_DEV, FW_DEV, D)
    output, unused = lax.scan(add_block, jnp.zeros((GROUP_TOKENS, D), jnp.float32), (blocks_hidden, blocks_weight))
    error = (output - target_rows.astype(jnp.float32)).astype(jnp.bfloat16)
    hidden_grad = lax.dot_general(weight_now, error, (((1,), (1,)), ((), ())), preferred_element_type=jnp.float32).astype(jnp.bfloat16)
    grad = jnp.dot(hidden_cols, error, preferred_element_type=jnp.float32) / GROUP_TOKENS
    weight_full = weight_now.astype(jnp.float32)
    first = 0.9 * moment_now.astype(jnp.float32) + 0.1 * grad
    secnd = 0.95 * second_now.astype(jnp.float32) + 0.05 * grad * grad
    stepped = first / corr_first / (jnp.sqrt(secnd / corr_second) + 1e-08)
    updated = (weight_full - 0.02 * (stepped + 0.1 * weight_full)).astype(jnp.bfloat16)
    return (updated, first.astype(jnp.bfloat16), hidden_grad)

def reference(hidden, target, weights, moment, second, round_index):
    updated, new_moment, hidden_grad = lax.map(one_group, (hidden, target, weights, moment, second))
    groups = jnp.arange(N_REP, dtype=jnp.int32)
    level = jnp.remainder(round_index[0].astype(jnp.int32), jnp.int32(LEVELS))
    partner = jnp.bitwise_xor(groups, jnp.left_shift(jnp.int32(1), level))
    partner_weights = jnp.take(updated, partner, axis=0)
    averaged = ((updated.astype(jnp.float32) + partner_weights.astype(jnp.float32)) * 0.5).astype(jnp.bfloat16)
    return (averaged, new_moment, hidden_grad)
```

```python
import functools

import jax
import jax.numpy as jnp
from jax import lax
from jax.experimental import pallas as pl
from jax.experimental.pallas import tpu as pltpu
from jax.sharding import PartitionSpec as P

MESH = pl.DeviceIdType.MESH
BF16 = jnp.bfloat16
F32 = jnp.float32
corr_first = 0.9999734386011124
corr_second = 0.994079470779666
NY = 4
NZ = 4
WIDTH = 128
LEVELS = 3


def f32(x):
    return x.astype(F32)


def kernel(
    level,
    h_hbm,
    t_hbm,
    w_hbm,
    m_hbm,
    s_hbm,
    avg_hbm,
    nm_hbm,
    hg_hbm,
    hid,
    hid_t,
    wts,
    mom,
    sec,
    tgt,
    part,
    got1,
    got2,
    got3,
    err,
    acc,
    upd,
    got6,
    avg,
    nmo,
    hgr,
    in_sem,
    out_sem,
    send_sem,
    recv_sem,
):
    chunks, units, width = wts.shape
    rows = tgt.shape[1]
    tokens = NY * NZ * rows
    block = NY * rows
    last = chunks - 1

    fs = lax.axis_index("fsdp")
    rep = lax.axis_index("rep")
    z = fs // NY
    y = fs % NY
    bit = 1 << level
    mate = {"rep": rep + bit * (1 - 2 * ((rep // bit) % 2))}
    yr = (y + 1) % NY
    yl = (y + 3) % NY
    y2 = (y + 2) % NY
    right = {"fsdp": z * NY + yr}
    left = {"fsdp": z * NY + yl}
    zs = [(z + k) % NZ for k in range(NZ)]
    zdev = [{"fsdp": zz * NY + y} for zz in zs]

    barrier = pltpu.get_barrier_semaphore()
    peers = [right, left, zdev[1], zdev[2], zdev[3], mate]
    for peer in peers:
        pl.semaphore_signal(barrier, inc=1, device_id=peer, device_id_type=MESH)

    def cols(c):
        return pl.ds(pl.multiple_of(c * width, width), width)

    sources = ((w_hbm, wts), (t_hbm, tgt), (m_hbm, mom), (s_hbm, sec))
    sinks = ((nmo, nm_hbm), (avg, avg_hbm))

    def load(c, j):
        src, dst = sources[j]
        return pltpu.make_async_copy(src.at[:, cols(c)], dst.at[c], in_sem.at[c, j])

    def write(c, j):
        src, dst = sinks[j]
        return pltpu.make_async_copy(src.at[c], dst.at[:, cols(c)], out_sem.at[c, j])

    load_h = pltpu.make_async_copy(h_hbm, hid, in_sem.at[0, 4])
    write_h = pltpu.make_async_copy(hgr, hg_hbm, out_sem.at[0, 2])

    def remote(src, dst, c, j, dev):
        return pltpu.make_async_remote_copy(
            src_ref=src,
            dst_ref=dst,
            send_sem=send_sem.at[c, j],
            recv_sem=recv_sem.at[c, j],
            device_id=dev,
            device_id_type=MESH,
        )

    lo = pl.ds(0, NZ // 2)
    hi = pl.ds(NZ // 2, NZ // 2)

    def ry_one(c):
        return [
            remote(part.at[c, lo, y2], got1.at[c, 0], c, 0, right),
            remote(part.at[c, hi, y2], got1.at[c, 1], c, 1, left),
        ]

    def ry_two(c):
        return [
            remote(part.at[c, :, yr], got2.at[c, 0], c, 2, right),
            remote(part.at[c, :, yl], got2.at[c, 1], c, 3, left),
        ]

    def rz(c):
        return [
            remote(part.at[c, zs[k], y], got3.at[c, k - 1], c, 3 + k, zdev[k])
            for k in (2, 1, 3)
        ]

    def gz(c):
        return [
            remote(err.at[c, z, y], err.at[c, z, y], c, 6 + k, zdev[k])
            for k in (2, 1, 3)
        ]

    def gy_one(c):
        return [
            remote(err.at[c, :, y], err.at[c, :, y], c, 10, right),
            remote(err.at[c, :, y], err.at[c, :, y], c, 11, left),
        ]

    def gy_two(c):
        return [
            remote(err.at[c, lo, yl], err.at[c, lo, yl], c, 12, right),
            remote(err.at[c, hi, yr], err.at[c, hi, yr], c, 13, left),
        ]

    def swap(c):
        return [remote(upd.at[c], got6.at[c], c, 14, mate)]

    def start(copies):
        for copy in copies:
            copy.start()

    def arrived(copies):
        for copy in copies:
            copy.wait_recv()

    load_h.start()

    @pl.loop(0, chunks)
    def _(c):
        for j in range(4):
            load(c, j).start()

    load_h.wait()

    for q in range(NZ):
        hid_t[q] = hid[:, q * block : (q + 1) * block].T

    def stage0(c):
        load(c, 0).wait()

        @pl.loop(0, NZ)
        def _(q):
            term = jnp.dot(hid_t[q], wts[c], preferred_element_type=F32)
            part[c, q] = term.astype(BF16).reshape(NY, rows, width)

        @pl.when(c == 0)
        def _():
            pl.semaphore_wait(barrier, len(peers))

        start(ry_one(c))

    def stage1(c):
        arrived(ry_one(c))
        part[c, lo, yr] = (f32(part[c, lo, yr]) + f32(got1[c, 0])).astype(BF16)
        part[c, hi, yl] = (f32(part[c, hi, yl]) + f32(got1[c, 1])).astype(BF16)
        start(ry_two(c))

    def stage2(c):
        arrived(ry_two(c))
        total = f32(part[c, :, y]) + f32(got2[c, 0]) + f32(got2[c, 1])
        part[c, :, y] = total.astype(BF16)
        start(rz(c))

    def stage3(c):
        load(c, 1).wait()
        arrived(rz(c))
        total = f32(part[c, z, y]) + f32(got3[c, 0])
        total += f32(got3[c, 1]) + f32(got3[c, 2])
        err[c, z, y] = (total - f32(tgt[c])).astype(BF16)
        start(gz(c))

    def stage4(c):
        arrived(gz(c))
        start(gy_one(c))

    def stage5(c):
        arrived(gy_one(c))
        start(gy_two(c))

    def stage6(c):
        arrived(gy_two(c))
        load(c, 2).wait()
        load(c, 3).wait()
        all_err = err[c].reshape(tokens, width)
        grad = jnp.dot(hid[...], all_err, preferred_element_type=F32) * (1.0 / tokens)
        weight = f32(wts[c])
        first = 0.9 * f32(mom[c]) + 0.1 * grad
        second = 0.95 * f32(sec[c]) + 0.05 * grad * grad
        step = (first * (1.0 / corr_first)) / (
            jnp.sqrt(second * (1.0 / corr_second)) + 1e-08
        )
        upd[c] = (weight - 0.02 * (step + 0.1 * weight)).astype(BF16)
        start(swap(c))
        nmo[c] = first.astype(BF16)
        write(c, 0).start()

        @pl.loop(0, NZ)
        def _(q):
            more = lax.dot_general(
                wts[c],
                err[c, q].reshape(block, width),
                (((1,), (1,)), ((), ())),
                preferred_element_type=F32,
            )

            @pl.when(c == 0)
            def _():
                acc[q] = more

            @pl.when(c > 0)
            def _():
                acc[q] += more

        @pl.when(c == last)
        def _():
            for q in range(NZ):
                hgr[:, q * block : (q + 1) * block] = acc[q].astype(BF16)
            write_h.start()

    def stage7(c):
        arrived(swap(c))
        avg[c] = ((f32(upd[c]) + f32(got6[c])) * 0.5).astype(BF16)
        write(c, 1).start()
        for copies in (ry_one, ry_two, rz, gz, gy_one, gy_two, swap):
            for copy in copies(c):
                copy.wait_send()

    stages = [stage0, stage1, stage2, stage3, stage4, stage5, stage6, stage7]

    @pl.loop(0, chunks + len(stages) - 1)
    def _(t):
        for k, stage in enumerate(stages):
            c = t - k

            @pl.when((c >= 0) & (c < chunks))
            def _(c=c, stage=stage):
                stage(c)

    write_h.wait()

    @pl.loop(0, chunks)
    def _(c):
        for j in range(2):
            write(c, j).wait()


def round_at(level, hidden, target, weights, moment, second):
    units, model = weights.shape
    tokens = hidden.shape[1]
    rows = target.shape[0]
    width = min(WIDTH, model)
    chunks = model // width
    block = NY * rows
    whole = jax.ShapeDtypeStruct((units, model), BF16)
    per_chunk = (chunks, units, width)
    return pl.pallas_call(
        functools.partial(kernel, level),
        out_shape=(whole, whole, jax.ShapeDtypeStruct((units, tokens), BF16)),
        in_specs=[pl.BlockSpec(memory_space=pl.ANY)] * 5,
        out_specs=[pl.BlockSpec(memory_space=pl.ANY)] * 3,
        scratch_shapes=[
            pltpu.VMEM((units, tokens), BF16),
            pltpu.VMEM((NZ, block, units), BF16),
            pltpu.VMEM(per_chunk, BF16),
            pltpu.VMEM(per_chunk, BF16),
            pltpu.VMEM(per_chunk, BF16),
            pltpu.VMEM((chunks, rows, width), BF16),
            pltpu.VMEM((chunks, NZ, NY, rows, width), BF16),
            pltpu.VMEM((chunks, 2, NZ // 2, rows, width), BF16),
            pltpu.VMEM((chunks, 2, NZ, rows, width), BF16),
            pltpu.VMEM((chunks, NZ - 1, rows, width), BF16),
            pltpu.VMEM((chunks, NZ, NY, rows, width), BF16),
            pltpu.VMEM((NZ, units, block), F32),
            pltpu.VMEM(per_chunk, BF16),
            pltpu.VMEM(per_chunk, BF16),
            pltpu.VMEM(per_chunk, BF16),
            pltpu.VMEM(per_chunk, BF16),
            pltpu.VMEM((units, tokens), BF16),
            pltpu.SemaphoreType.DMA((chunks, 5)),
            pltpu.SemaphoreType.DMA((chunks, 3)),
            pltpu.SemaphoreType.DMA((chunks, 15)),
            pltpu.SemaphoreType.DMA((chunks, 15)),
        ],
        compiler_params=pltpu.CompilerParams(
            collective_id=level,
            has_side_effects=True,
            vmem_limit_bytes=60 * 1024 * 1024,
        ),
    )(hidden, target, weights, moment, second)


def local(hidden, target, weights, moment, second, round_index):
    levels = 1
    while levels < LEVELS and 2 << levels <= lax.axis_size("rep"):
        levels += 1
    branches = [functools.partial(round_at, level) for level in range(levels)]
    chosen = jnp.remainder(round_index[0], levels)
    averaged, new_moment, hidden_grad = lax.switch(
        chosen, branches, hidden[0], target[0], weights[0], moment[0], second[0]
    )
    return (averaged[None], new_moment[None], hidden_grad[None])


def solution(mesh):
    split = P("rep", "fsdp", None)
    return jax.shard_map(
        local,
        mesh=mesh,
        in_specs=(split,) * 5 + (P(),),
        out_specs=(split,) * 3,
        check_vma=False,
    )
```

```python
import functools

import jax
import jax.numpy as jnp
from jax import lax
from jax.experimental import pallas as pl
from jax.experimental.pallas import tpu as pltpu
from jax.sharding import PartitionSpec as P

MESH = pl.DeviceIdType.MESH
BF16 = jnp.bfloat16
F32 = jnp.float32
corr_first = 0.9999734386011124
corr_second = 0.994079470779666
NY = 4
NZ = 4
WIDTH = 128
SIDE = 32
LEVELS = 3


def f32(x):
    return x.astype(F32)


def kernel(
    level,
    h_hbm,
    t_hbm,
    w_hbm,
    m_hbm,
    s_hbm,
    avg_hbm,
    nm_hbm,
    hg_hbm,
    hid,
    hid_t,
    wts,
    mom,
    sec,
    tgt,
    part,
    got1,
    got2,
    main_got,
    main_fwd,
    side_got,
    side_fwd,
    got5,
    err,
    acc,
    upd,
    got6,
    avg,
    nmo,
    hgr,
    in_sem,
    out_sem,
    send_sem,
    recv_sem,
):
    chunks, units, width = wts.shape
    rows = tgt.shape[1]
    tokens = NY * NZ * rows
    block = NY * rows
    last = chunks - 1
    main = pl.ds(0, rows - SIDE)
    side = pl.ds(rows - SIDE, SIDE)

    fs = lax.axis_index("fsdp")
    rep = lax.axis_index("rep")
    z = fs // NY
    y = fs % NY
    bit = 1 << level
    mate = {"rep": rep + bit * (1 - 2 * ((rep // bit) % 2))}
    yr = (y + 1) % NY
    yl = (y + 3) % NY
    y2 = (y + 2) % NY
    right = {"fsdp": z * NY + yr}
    left = {"fsdp": z * NY + yl}
    end = z % 3 == 0
    inner = z % 3 > 0
    near, mid = 1 + z // 3, 2 - z // 3
    outer, twin, far = 3 * (z - 1), 3 - z, 3 * (2 - z)
    beyond = pl.ds(2 - 2 * (z // 3), 2)
    across = pl.ds(4 - 2 * z, 2)
    ys = [y, yr, y2, yl]
    ydev = [{"fsdp": z * NY + yy} for yy in ys]

    barrier = pltpu.get_barrier_semaphore()
    zpeers = [{"fsdp": (z + k) % NZ * NY + y} for k in range(1, NZ)]
    peers = [right, left, ydev[2], mate] + zpeers
    for peer in peers:
        pl.semaphore_signal(barrier, inc=1, device_id=peer, device_id_type=MESH)

    def cols(c):
        return pl.ds(pl.multiple_of(c * width, width), width)

    sources = ((w_hbm, wts), (t_hbm, tgt), (m_hbm, mom), (s_hbm, sec))
    sinks = ((nmo, nm_hbm), (avg, avg_hbm))

    def load(c, j):
        src, dst = sources[j]
        return pltpu.make_async_copy(src.at[:, cols(c)], dst.at[c], in_sem.at[c, j])

    def write(c, j):
        src, dst = sinks[j]
        return pltpu.make_async_copy(src.at[c], dst.at[:, cols(c)], out_sem.at[c, j])

    load_h = pltpu.make_async_copy(h_hbm, hid, in_sem.at[0, 4])
    write_h = pltpu.make_async_copy(hgr, hg_hbm, out_sem.at[0, 2])

    def remote(src, dst, c, j, dev, k=None):
        return pltpu.make_async_remote_copy(
            src_ref=src,
            dst_ref=dst,
            send_sem=send_sem.at[c, j],
            recv_sem=recv_sem.at[c, j if k is None else k],
            device_id=dev,
            device_id_type=MESH,
        )

    lo = pl.ds(0, NZ // 2)
    hi = pl.ds(NZ // 2, NZ // 2)

    def ry_one(c):
        return [
            remote(part.at[c, lo, y2, main], got1.at[c, 0], c, 0, right),
            remote(part.at[c, hi, y2, main], got1.at[c, 1], c, 1, left),
        ]

    def ry_two(c):
        return [
            remote(part.at[c, :, yr, main], got2.at[c, 0], c, 2, right),
            remote(part.at[c, :, yl, main], got2.at[c, 1], c, 3, left),
        ]

    def gy_one(c):
        own = err.at[c, :, y, main]
        return [remote(own, own, c, 4, right), remote(own, own, c, 5, left)]

    def gy_two(c):
        one = err.at[c, lo, yl, main]
        two = err.at[c, hi, yr, main]
        return [remote(one, one, c, 6, right), remote(two, two, c, 7, left)]

    def side_ry(c):
        return [
            remote(part.at[c, z, ys[k], side], got5.at[c, k - 1], c, 8 + k, ydev[k])
            for k in (2, 1, 3)
        ]

    def side_gy(c):
        own = err.at[c, z, y, side]
        return [remote(own, own, c, 11 + k, ydev[k]) for k in (2, 1, 3)]

    def swap(c):
        return [remote(upd.at[c], got6.at[c], c, 8, mate)]

    sends = (ry_one, ry_two, gy_one, gy_two, swap, side_ry, side_gy)

    def start(copies):
        for copy in copies:
            copy.start()

    def arrived(copies):
        for copy in copies:
            copy.wait_recv()

    def zdev(zz):
        return {"fsdp": zz * NY + y}

    class Line:
        def __init__(self, view, got, fwd, base):
            self.view, self.got, self.fwd, self.base = view, got, fwd, base

        def move(self, src, dst, c, j, k, zz):
            return remote(src, dst, c, self.base + j, zdev(zz), self.base + k)

        def sum_end(self, c):
            two, one = self.view(part, c, beyond), self.view(part, c, near)
            return [
                self.move(two, self.fwd.at[c], c, 0, 0, near),
                self.move(one, self.got.at[c, 0], c, 1, 1, near),
            ]

        def sum_inner(self, c):
            one = self.view(part, c, outer)
            return [self.move(one, self.got.at[c, 0], c, 1, 1, outer)]

        def sum_on(self, c):
            one, two = self.view(part, c, far), self.view(part, c, twin)
            return [
                self.move(one, self.got.at[c, 1], c, 3, 2, far),
                self.move(two, self.got.at[c, 1], c, 2, 2, twin),
            ]

        def sum_start(self, c):
            @pl.when(end)
            def _():
                start(self.sum_end(c))

            @pl.when(inner)
            def _():
                start(self.sum_inner(c))

        def sum_forward(self, c):
            @pl.when(inner)
            def _():
                two = self.view(part, c, across)
                self.move(two, self.fwd.at[c], c, 0, 0, outer).wait_recv()
                two[...] = (f32(two[...]) + f32(self.fwd[c])).astype(BF16)
                start(self.sum_on(c))

        def sum_finish(self, c):
            own = self.view(part, c, z)
            for k in range(2):
                got = self.got.at[c, k]
                self.move(got, got, c, 1 + k, 1 + k, twin).wait_recv()
            return f32(own[...]) + f32(self.got[c, 0]) + f32(self.got[c, 1])

        def share_end(self, c):
            own = self.view(err, c, z)
            return [
                self.move(own, own, c, 4, 6, mid),
                self.move(own, own, c, 5, 4, near),
            ]

        def share_inner(self, c):
            own = self.view(err, c, z)
            return [
                self.move(own, own, c, 4, 5, twin),
                self.move(own, own, c, 5, 4, outer),
            ]

        def share_on(self, c):
            two = self.view(err, c, across)
            return [self.move(two, two, c, 6, 7, outer)]

        def share_start(self, c):
            @pl.when(end)
            def _():
                start(self.share_end(c))

            @pl.when(inner)
            def _():
                start(self.share_inner(c))

        def share_forward(self, c):
            own = self.view(err, c, z)
            self.move(own, own, c, 4, 4, twin).wait_recv()

            @pl.when(inner)
            def _():
                for k in (5, 6):
                    self.move(own, own, c, 4, k, twin).wait_recv()
                start(self.share_on(c))

        def share_finish(self, c):
            @pl.when(end)
            def _():
                two = self.view(err, c, beyond)
                self.move(two, two, c, 6, 7, twin).wait_recv()

        def sent(self, c):
            @pl.when(end)
            def _():
                for copy in self.sum_end(c) + self.share_end(c):
                    copy.wait_send()

            @pl.when(inner)
            def _():
                copies = self.sum_inner(c) + self.sum_on(c)
                for copy in copies + self.share_inner(c) + self.share_on(c):
                    copy.wait_send()

    def main_view(ref, c, zz):
        return ref.at[c, zz, y, main]

    def side_view(ref, c, zz):
        return ref.at[c, zz, :, side]

    main_line = Line(main_view, main_got, main_fwd, 15)
    side_line = Line(side_view, side_got, side_fwd, 23)

    load_h.start()
    load(0, 0).start()
    load_h.wait()

    @pl.loop(1, chunks)
    def _(c):
        load(c, 0).start()

    @pl.loop(0, chunks)
    def _(c):
        for j in range(1, 4):
            load(c, j).start()

    for q in range(NZ):
        hid_t[q] = hid[:, q * block : (q + 1) * block].T

    def stage0(c):
        load(c, 0).wait()

        @pl.loop(0, NZ)
        def _(q):
            term = jnp.dot(hid_t[q], wts[c], preferred_element_type=F32)
            part[c, q] = term.astype(BF16).reshape(NY, rows, width)

        @pl.when(c == 0)
        def _():
            pl.semaphore_wait(barrier, len(peers))

        start(ry_one(c))
        side_line.sum_start(c)

    def stage1(c):
        arrived(ry_one(c))
        part[c, lo, yr, main] = (f32(part[c, lo, yr, main]) + f32(got1[c, 0])).astype(BF16)
        part[c, hi, yl, main] = (f32(part[c, hi, yl, main]) + f32(got1[c, 1])).astype(BF16)
        start(ry_two(c))
        side_line.sum_forward(c)

    def stage2(c):
        total = side_line.sum_finish(c)
        part[c, z, :, side] = total.astype(BF16)
        start(side_ry(c))
        arrived(ry_two(c))
        total = f32(part[c, :, y, main]) + f32(got2[c, 0]) + f32(got2[c, 1])
        part[c, :, y, main] = total.astype(BF16)
        main_line.sum_start(c)

    def stage3(c):
        load(c, 1).wait()
        arrived(side_ry(c))
        total = f32(part[c, z, y, side]) + f32(got5[c, 0])
        total += f32(got5[c, 1]) + f32(got5[c, 2])
        err[c, z, y, side] = (total - f32(tgt[c, side])).astype(BF16)
        start(side_gy(c))
        main_line.sum_forward(c)

    def stage4(c):
        arrived(side_gy(c))
        side_line.share_start(c)
        total = main_line.sum_finish(c)
        err[c, z, y, main] = (total - f32(tgt[c, main])).astype(BF16)
        main_line.share_start(c)

    def stage5(c):
        side_line.share_forward(c)
        main_line.share_forward(c)

    def stage6(c):
        main_line.share_finish(c)
        start(gy_one(c))

    def stage7(c):
        arrived(gy_one(c))
        start(gy_two(c))

    def stage8(c):
        side_line.share_finish(c)
        arrived(gy_two(c))
        load(c, 2).wait()
        load(c, 3).wait()
        all_err = err[c].reshape(tokens, width)
        grad = jnp.dot(hid[...], all_err, preferred_element_type=F32) * (1.0 / tokens)
        weight = f32(wts[c])
        first = 0.9 * f32(mom[c]) + 0.1 * grad
        second = 0.95 * f32(sec[c]) + 0.05 * grad * grad
        step = (first * (1.0 / corr_first)) / (
            jnp.sqrt(second * (1.0 / corr_second)) + 1e-08
        )
        upd[c] = (weight - 0.02 * (step + 0.1 * weight)).astype(BF16)
        start(swap(c))
        nmo[c] = first.astype(BF16)
        write(c, 0).start()

        @pl.loop(0, NZ)
        def _(q):
            more = lax.dot_general(
                wts[c],
                err[c, q].reshape(block, width),
                (((1,), (1,)), ((), ())),
                preferred_element_type=F32,
            )

            @pl.when(c == 0)
            def _():
                acc[q] = more

            @pl.when(c > 0)
            def _():
                acc[q] += more

        @pl.when(c == last)
        def _():
            for q in range(NZ):
                hgr[:, q * block : (q + 1) * block] = acc[q].astype(BF16)
            write_h.start()

    def stage9(c):
        arrived(swap(c))
        avg[c] = ((f32(upd[c]) + f32(got6[c])) * 0.5).astype(BF16)
        write(c, 1).start()
        main_line.sent(c)
        side_line.sent(c)
        for copies in sends:
            for copy in copies(c):
                copy.wait_send()

    stages = (
        (0, stage0),
        (2, stage1),
        (4, stage2),
        (6, stage3),
        (8, stage4),
        (10, stage5),
        (12, stage6),
        (14, stage7),
        (16, stage8),
        (18, stage9),
    )

    @pl.loop(0, chunks + stages[-1][0])
    def _(t):
        for lag, stage in stages:
            c = t - lag

            @pl.when((c >= 0) & (c < chunks))
            def _(c=c, stage=stage):
                stage(c)

    write_h.wait()

    @pl.loop(0, chunks)
    def _(c):
        for j in range(2):
            write(c, j).wait()


def round_at(level, hidden, target, weights, moment, second):
    units, model = weights.shape
    tokens = hidden.shape[1]
    rows = target.shape[0]
    width = min(WIDTH, model)
    chunks = model // width
    block = NY * rows
    whole = jax.ShapeDtypeStruct((units, model), BF16)
    per_chunk = (chunks, units, width)
    return pl.pallas_call(
        functools.partial(kernel, level),
        out_shape=(whole, whole, jax.ShapeDtypeStruct((units, tokens), BF16)),
        in_specs=[pl.BlockSpec(memory_space=pl.ANY)] * 5,
        out_specs=[pl.BlockSpec(memory_space=pl.ANY)] * 3,
        scratch_shapes=[
            pltpu.VMEM((units, tokens), BF16),
            pltpu.VMEM((NZ, block, units), BF16),
            pltpu.VMEM(per_chunk, BF16),
            pltpu.VMEM(per_chunk, BF16),
            pltpu.VMEM(per_chunk, BF16),
            pltpu.VMEM((chunks, rows, width), BF16),
            pltpu.VMEM((chunks, NZ, NY, rows, width), BF16),
            pltpu.VMEM((chunks, 2, NZ // 2, rows - SIDE, width), BF16),
            pltpu.VMEM((chunks, 2, NZ, rows - SIDE, width), BF16),
            pltpu.VMEM((chunks, 2, rows - SIDE, width), BF16),
            pltpu.VMEM((chunks, 2, rows - SIDE, width), BF16),
            pltpu.VMEM((chunks, 2, NY, SIDE, width), BF16),
            pltpu.VMEM((chunks, 2, NY, SIDE, width), BF16),
            pltpu.VMEM((chunks, NY - 1, SIDE, width), BF16),
            pltpu.VMEM((chunks, NZ, NY, rows, width), BF16),
            pltpu.VMEM((NZ, units, block), F32),
            pltpu.VMEM(per_chunk, BF16),
            pltpu.VMEM(per_chunk, BF16),
            pltpu.VMEM(per_chunk, BF16),
            pltpu.VMEM(per_chunk, BF16),
            pltpu.VMEM((units, tokens), BF16),
            pltpu.SemaphoreType.DMA((chunks, 5)),
            pltpu.SemaphoreType.DMA((chunks, 3)),
            pltpu.SemaphoreType.DMA((chunks, 31)),
            pltpu.SemaphoreType.DMA((chunks, 31)),
        ],
        compiler_params=pltpu.CompilerParams(
            collective_id=level,
            has_side_effects=True,
            vmem_limit_bytes=50 * 1024 * 1024,
        ),
    )(hidden, target, weights, moment, second)


def local(hidden, target, weights, moment, second, round_index):
    levels = 1
    while levels < LEVELS and 2 << levels <= lax.axis_size("rep"):
        levels += 1
    branches = [functools.partial(round_at, level) for level in range(levels)]
    chosen = jnp.remainder(round_index[0], levels)
    averaged, new_moment, hidden_grad = lax.switch(
        chosen, branches, hidden[0], target[0], weights[0], moment[0], second[0]
    )
    return (averaged[None], new_moment[None], hidden_grad[None])


def solution(mesh):
    split = P("rep", "fsdp", None)
    return jax.shard_map(
        local,
        mesh=mesh,
        in_specs=(split,) * 5 + (P(),),
        out_specs=(split,) * 3,
        check_vma=False,
    )
```

```python
import functools

import jax
import jax.numpy as jnp
from jax import lax
from jax.experimental import pallas as pl
from jax.experimental.pallas import tpu as pltpu
from jax.sharding import PartitionSpec as P

MESH = pl.DeviceIdType.MESH
BF16 = jnp.bfloat16
F32 = jnp.float32
corr_first = 0.9999734386011124
corr_second = 0.994079470779666
NY = 4
NZ = 4
WIDTH = 256
SIDE = 32
LEVELS = 3


def f32(x):
    return x.astype(F32)


def kernel(
    level,
    h_hbm,
    t_hbm,
    w_hbm,
    m_hbm,
    s_hbm,
    avg_hbm,
    nm_hbm,
    hg_hbm,
    hid,
    hid_t,
    wts,
    mom,
    sec,
    tgt,
    part,
    got1,
    got2,
    main_got,
    main_fwd,
    side_got,
    side_fwd,
    got5,
    err,
    acc,
    gsum,
    upd,
    got6,
    avg,
    nmo,
    hgr,
    in_sem,
    out_sem,
    send_sem,
    recv_sem,
):
    chunks, units, width = wts.shape
    rows = tgt.shape[1]
    tokens = NY * NZ * rows
    block = NY * rows
    last = chunks - 1
    main = pl.ds(0, rows - SIDE)
    side = pl.ds(rows - SIDE, SIDE)

    fs = lax.axis_index("fsdp")
    rep = lax.axis_index("rep")
    z = fs // NY
    y = fs % NY
    bit = 1 << level
    mate = {"rep": rep + bit * (1 - 2 * ((rep // bit) % 2))}
    yr = (y + 1) % NY
    yl = (y + 3) % NY
    y2 = (y + 2) % NY
    right = {"fsdp": z * NY + yr}
    left = {"fsdp": z * NY + yl}
    end = z % 3 == 0
    inner = z % 3 > 0
    near, mid = 1 + z // 3, 2 - z // 3
    outer, twin, far = 3 * (z - 1), 3 - z, 3 * (2 - z)
    beyond = pl.ds(2 - 2 * (z // 3), 2)
    across = pl.ds(4 - 2 * z, 2)
    ys = [y, yr, y2, yl]
    ydev = [{"fsdp": z * NY + yy} for yy in ys]

    barrier = pltpu.get_barrier_semaphore()
    zpeers = [{"fsdp": (z + k) % NZ * NY + y} for k in range(1, NZ)]
    peers = [right, left, ydev[2], mate] + zpeers
    for peer in peers:
        pl.semaphore_signal(barrier, inc=1, device_id=peer, device_id_type=MESH)

    def cols(c):
        return pl.ds(pl.multiple_of(c * width, width), width)

    sources = ((w_hbm, wts), (t_hbm, tgt), (m_hbm, mom), (s_hbm, sec))
    sinks = ((nmo, nm_hbm), (avg, avg_hbm))

    def load(c, j):
        src, dst = sources[j]
        return pltpu.make_async_copy(src.at[:, cols(c)], dst.at[c], in_sem.at[c, j])

    def write(c, j):
        src, dst = sinks[j]
        return pltpu.make_async_copy(src.at[c], dst.at[:, cols(c)], out_sem.at[c, j])

    def load_h(q):
        some = pl.ds(q * block, block)
        return pltpu.make_async_copy(h_hbm.at[:, some], hid.at[:, some], in_sem.at[q, 4])

    write_h = pltpu.make_async_copy(hgr, hg_hbm, out_sem.at[0, 2])

    def remote(src, dst, c, j, dev, k=None):
        return pltpu.make_async_remote_copy(
            src_ref=src,
            dst_ref=dst,
            send_sem=send_sem.at[c, j],
            recv_sem=recv_sem.at[c, j if k is None else k],
            device_id=dev,
            device_id_type=MESH,
        )

    lo = pl.ds(0, NZ // 2)
    hi = pl.ds(NZ // 2, NZ // 2)

    def ry_one(c):
        return [
            remote(part.at[c, lo, y2, main], got1.at[c, 0], c, 0, right),
            remote(part.at[c, hi, y2, main], got1.at[c, 1], c, 1, left),
        ]

    def ry_two(c):
        return [
            remote(part.at[c, :, yr, main], got2.at[c, 0], c, 2, right),
            remote(part.at[c, :, yl, main], got2.at[c, 1], c, 3, left),
        ]

    def gy_one(c):
        own = err.at[c, :, y, main]
        return [remote(own, own, c, 4, right), remote(own, own, c, 5, left)]

    def gy_two(c):
        one = err.at[c, lo, yl, main]
        two = err.at[c, hi, yr, main]
        return [remote(one, one, c, 6, right), remote(two, two, c, 7, left)]

    def side_ry(c):
        return [
            remote(part.at[c, z, ys[k], side], got5.at[c, k - 1], c, 8 + k, ydev[k])
            for k in (2, 1, 3)
        ]

    def side_gy(c):
        own = err.at[c, z, y, side]
        return [remote(own, own, c, 11 + k, ydev[k]) for k in (2, 1, 3)]

    half = units // 2
    halves = [pl.ds(0, half), pl.ds(half, half)]

    def swap(c):
        return [
            remote(upd.at[c, part_rows], got6.at[c, part_rows], c, j, mate)
            for part_rows, j in zip(halves, (8, 31))
        ]

    sends = (ry_one, ry_two, gy_one, gy_two, swap, side_ry, side_gy)

    def start(copies):
        for copy in copies:
            copy.start()

    def arrived(copies):
        for copy in copies:
            copy.wait_recv()

    def zdev(zz):
        return {"fsdp": zz * NY + y}

    class Line:
        def __init__(self, view, got, fwd, base):
            self.view, self.got, self.fwd, self.base = view, got, fwd, base

        def move(self, src, dst, c, j, k, zz):
            return remote(src, dst, c, self.base + j, zdev(zz), self.base + k)

        def sum_end(self, c):
            two, one = self.view(part, c, beyond), self.view(part, c, near)
            return [
                self.move(two, self.fwd.at[c], c, 0, 0, near),
                self.move(one, self.got.at[c, 0], c, 1, 1, near),
            ]

        def sum_inner(self, c):
            one = self.view(part, c, outer)
            return [self.move(one, self.got.at[c, 0], c, 1, 1, outer)]

        def sum_on(self, c):
            one, two = self.view(part, c, far), self.view(part, c, twin)
            return [
                self.move(one, self.got.at[c, 1], c, 3, 2, far),
                self.move(two, self.got.at[c, 1], c, 2, 2, twin),
            ]

        def sum_start(self, c):
            @pl.when(end)
            def _():
                start(self.sum_end(c))

            @pl.when(inner)
            def _():
                start(self.sum_inner(c))

        def sum_forward(self, c):
            @pl.when(inner)
            def _():
                two = self.view(part, c, across)
                self.move(two, self.fwd.at[c], c, 0, 0, outer).wait_recv()
                two[...] = (f32(two[...]) + f32(self.fwd[c])).astype(BF16)
                start(self.sum_on(c))

        def sum_finish(self, c):
            own = self.view(part, c, z)
            for k in range(2):
                got = self.got.at[c, k]
                self.move(got, got, c, 1 + k, 1 + k, twin).wait_recv()
            return f32(own[...]) + f32(self.got[c, 0]) + f32(self.got[c, 1])

        def share_end(self, c):
            own = self.view(err, c, z)
            return [
                self.move(own, own, c, 4, 6, mid),
                self.move(own, own, c, 5, 4, near),
            ]

        def share_inner(self, c):
            own = self.view(err, c, z)
            return [
                self.move(own, own, c, 4, 5, twin),
                self.move(own, own, c, 5, 4, outer),
            ]

        def share_on(self, c):
            two = self.view(err, c, across)
            return [self.move(two, two, c, 6, 7, outer)]

        def share_start(self, c):
            @pl.when(end)
            def _():
                start(self.share_end(c))

            @pl.when(inner)
            def _():
                start(self.share_inner(c))

        def share_forward(self, c):
            own = self.view(err, c, z)
            self.move(own, own, c, 4, 4, twin).wait_recv()

            @pl.when(inner)
            def _():
                for k in (5, 6):
                    self.move(own, own, c, 4, k, twin).wait_recv()
                start(self.share_on(c))

        def share_finish(self, c):
            @pl.when(end)
            def _():
                two = self.view(err, c, beyond)
                self.move(two, two, c, 6, 7, twin).wait_recv()

        def sent(self, c):
            @pl.when(end)
            def _():
                for copy in self.sum_end(c) + self.share_end(c):
                    copy.wait_send()

            @pl.when(inner)
            def _():
                copies = self.sum_inner(c) + self.sum_on(c)
                for copy in copies + self.share_inner(c) + self.share_on(c):
                    copy.wait_send()

    def main_view(ref, c, zz):
        return ref.at[c, zz, y, main]

    def side_view(ref, c, zz):
        return ref.at[c, zz, :, side]

    main_line = Line(main_view, main_got, main_fwd, 15)
    side_line = Line(side_view, side_got, side_fwd, 23)

    load(0, 0).start()
    for q in range(NZ):
        load_h(q).start()

    @pl.loop(1, chunks)
    def _(c):
        load(c, 0).start()

    @pl.loop(0, chunks)
    def _(c):
        for j in range(1, 4):
            load(c, j).start()

    def stage0(c):
        load(c, 0).wait()

        @pl.when(c == 0)
        def _():
            for q in range(NZ):
                load_h(q).wait()
                hid_t[q] = hid[:, q * block : (q + 1) * block].T

        @pl.loop(0, NZ)
        def _(q):
            term = jnp.dot(hid_t[q], wts[c], preferred_element_type=F32)
            part[c, q] = term.astype(BF16).reshape(NY, rows, width)

        @pl.when(c == 0)
        def _():
            pl.semaphore_wait(barrier, len(peers))

        start(ry_one(c))
        side_line.sum_start(c)

    def stage1(c):
        arrived(ry_one(c))
        part[c, lo, yr, main] = (f32(part[c, lo, yr, main]) + f32(got1[c, 0])).astype(BF16)
        part[c, hi, yl, main] = (f32(part[c, hi, yl, main]) + f32(got1[c, 1])).astype(BF16)
        start(ry_two(c))
        side_line.sum_forward(c)

    def stage2(c):
        total = side_line.sum_finish(c)
        part[c, z, :, side] = total.astype(BF16)
        start(side_ry(c))
        arrived(ry_two(c))
        total = f32(part[c, :, y, main]) + f32(got2[c, 0]) + f32(got2[c, 1])
        part[c, :, y, main] = total.astype(BF16)
        main_line.sum_start(c)

    def stage3(c):
        load(c, 1).wait()
        arrived(side_ry(c))
        total = f32(part[c, z, y, side]) + f32(got5[c, 0])
        total += f32(got5[c, 1]) + f32(got5[c, 2])
        err[c, z, y, side] = (total - f32(tgt[c, side])).astype(BF16)
        start(side_gy(c))
        main_line.sum_forward(c)

    def stage4(c):
        arrived(side_gy(c))
        side_line.share_start(c)
        total = main_line.sum_finish(c)
        err[c, z, y, main] = (total - f32(tgt[c, main])).astype(BF16)
        main_line.share_start(c)

    def stage5(c):
        side_line.share_forward(c)
        main_line.share_forward(c)

    def stage6(c):
        main_line.share_finish(c)
        start(gy_one(c))

    def stage7(c):
        arrived(gy_one(c))
        start(gy_two(c))

    def stage8(c):
        side_line.share_finish(c)
        arrived(gy_two(c))
        load(c, 2).wait()
        load(c, 3).wait()
        all_err = err[c].reshape(tokens, width)
        for move, some in zip(swap(c), halves):
            grad = jnp.dot(hid[some], all_err, preferred_element_type=F32)
            grad = grad * (1.0 / tokens)
            weight = f32(wts[c, some])
            first = 0.9 * f32(mom[c, some]) + 0.1 * grad
            second = 0.95 * f32(sec[c, some]) + 0.05 * grad * grad
            step = (first * (1.0 / corr_first)) / (
                jnp.sqrt(second * (1.0 / corr_second)) + 1e-08
            )
            upd[c, some] = (weight - 0.02 * (step + 0.1 * weight)).astype(BF16)
            move.start()
            nmo[c, some] = first.astype(BF16)
        write(c, 0).start()

        @pl.when(c == 0)
        def _():
            acc[...] = jnp.zeros_like(acc)

        @pl.loop(0, NZ)
        def _(q):
            acc[q] += lax.dot_general(
                wts[c],
                err[c, q].reshape(block, width),
                (((1,), (1,)), ((), ())),
                preferred_element_type=F32,
            )

        @pl.when(c == last)
        def _():
            for q in range(NZ):
                hgr[:, q * block : (q + 1) * block] = acc[q].astype(BF16)
            write_h.start()

    def stage9(c):
        for move, some in zip(swap(c), halves):
            move.wait_recv()
            both = f32(upd[c, some]) + f32(got6[c, some])
            avg[c, some] = (both * 0.5).astype(BF16)
        write(c, 1).start()
        main_line.sent(c)
        side_line.sent(c)
        for copies in sends:
            for copy in copies(c):
                copy.wait_send()

    stages = (
        (0, stage0),
        (1, stage1),
        (2, stage2),
        (3, stage3),
        (4, stage4),
        (5, stage5),
        (6, stage6),
        (7, stage7),
        (8, stage8),
        (9, stage9),
    )

    @pl.loop(0, chunks + 9)
    def _(t):
        for lag, stage in stages:
            c = t - lag

            @pl.when((c >= 0) & (c < chunks))
            def _(c=c, stage=stage):
                stage(c)

    write_h.wait()

    @pl.loop(0, chunks)
    def _(c):
        for j in range(2):
            write(c, j).wait()


def round_at(level, hidden, target, weights, moment, second):
    units, model = weights.shape
    tokens = hidden.shape[1]
    rows = target.shape[0]
    width = min(WIDTH, model)
    chunks = model // width
    block = NY * rows
    whole = jax.ShapeDtypeStruct((units, model), BF16)
    per_chunk = (chunks, units, width)
    return pl.pallas_call(
        functools.partial(kernel, level),
        out_shape=(whole, whole, jax.ShapeDtypeStruct((units, tokens), BF16)),
        in_specs=[pl.BlockSpec(memory_space=pl.ANY)] * 5,
        out_specs=[pl.BlockSpec(memory_space=pl.ANY)] * 3,
        scratch_shapes=[
            pltpu.VMEM((units, tokens), BF16),
            pltpu.VMEM((NZ, block, units), BF16),
            pltpu.VMEM(per_chunk, BF16),
            pltpu.VMEM(per_chunk, BF16),
            pltpu.VMEM(per_chunk, BF16),
            pltpu.VMEM((chunks, rows, width), BF16),
            pltpu.VMEM((chunks, NZ, NY, rows, width), BF16),
            pltpu.VMEM((chunks, 2, NZ // 2, rows - SIDE, width), BF16),
            pltpu.VMEM((chunks, 2, NZ, rows - SIDE, width), BF16),
            pltpu.VMEM((chunks, 2, rows - SIDE, width), BF16),
            pltpu.VMEM((chunks, 2, rows - SIDE, width), BF16),
            pltpu.VMEM((chunks, 2, NY, SIDE, width), BF16),
            pltpu.VMEM((chunks, 2, NY, SIDE, width), BF16),
            pltpu.VMEM((chunks, NY - 1, SIDE, width), BF16),
            pltpu.VMEM((chunks, NZ, NY, rows, width), BF16),
            pltpu.VMEM((NZ, units, block), F32),
            pltpu.VMEM((units, width), F32),
            pltpu.VMEM(per_chunk, BF16),
            pltpu.VMEM(per_chunk, BF16),
            pltpu.VMEM(per_chunk, BF16),
            pltpu.VMEM(per_chunk, BF16),
            pltpu.VMEM((units, tokens), BF16),
            pltpu.SemaphoreType.DMA((max(chunks, NZ), 5)),
            pltpu.SemaphoreType.DMA((chunks, 3)),
            pltpu.SemaphoreType.DMA((chunks, 32)),
            pltpu.SemaphoreType.DMA((chunks, 32)),
        ],
        compiler_params=pltpu.CompilerParams(
            collective_id=level,
            has_side_effects=True,
            vmem_limit_bytes=50 * 1024 * 1024,
        ),
    )(hidden, target, weights, moment, second)


def local(hidden, target, weights, moment, second, round_index):
    levels = 1
    while levels < LEVELS and 2 << levels <= lax.axis_size("rep"):
        levels += 1
    branches = [functools.partial(round_at, level) for level in range(levels)]
    chosen = jnp.remainder(round_index[0], levels)
    averaged, new_moment, hidden_grad = lax.switch(
        chosen, branches, hidden[0], target[0], weights[0], moment[0], second[0]
    )
    return (averaged[None], new_moment[None], hidden_grad[None])


def solution(mesh):
    split = P("rep", "fsdp", None)
    return jax.shard_map(
        local,
        mesh=mesh,
        in_specs=(split,) * 5 + (P(),),
        out_specs=(split,) * 3,
        check_vma=False,
    )
```

```python
import functools

import jax
import jax.numpy as jnp
from jax import lax
from jax.experimental import pallas as pl
from jax.experimental.pallas import tpu as pltpu
from jax.sharding import PartitionSpec as P

MESH = pl.DeviceIdType.MESH
BF16 = jnp.bfloat16
F32 = jnp.float32
corr_first = 0.9999734386011124
corr_second = 0.994079470779666
NY = 4
NZ = 4
WIDTH = 256
SIDE = 32
LEVELS = 3


def f32(x):
    return x.astype(F32)


def kernel(
    level,
    h_hbm,
    t_hbm,
    w_hbm,
    m_hbm,
    s_hbm,
    avg_hbm,
    nm_hbm,
    hg_hbm,
    hid,
    hid_t,
    wts,
    mom,
    sec,
    tgt,
    part,
    got1,
    got2,
    main_got,
    main_fwd,
    side_got,
    side_fwd,
    got5,
    err,
    acc,
    gsum,
    upd,
    got6,
    avg,
    nmo,
    hgr,
    in_sem,
    out_sem,
    send_sem,
    recv_sem,
):
    chunks, units, width = wts.shape
    rows = tgt.shape[1]
    tokens = NY * NZ * rows
    block = NY * rows
    last = chunks - 1
    main = pl.ds(0, rows - SIDE)
    side = pl.ds(rows - SIDE, SIDE)

    fs = lax.axis_index("fsdp")
    rep = lax.axis_index("rep")
    z = fs // NY
    y = fs % NY
    bit = 1 << level
    mate = {"rep": rep + bit * (1 - 2 * ((rep // bit) % 2))}
    yr = (y + 1) % NY
    yl = (y + 3) % NY
    y2 = (y + 2) % NY
    right = {"fsdp": z * NY + yr}
    left = {"fsdp": z * NY + yl}
    end = z % 3 == 0
    inner = z % 3 > 0
    near, mid = 1 + z // 3, 2 - z // 3
    outer, twin, far = 3 * (z - 1), 3 - z, 3 * (2 - z)
    beyond = pl.ds(2 - 2 * (z // 3), 2)
    across = pl.ds(4 - 2 * z, 2)
    ys = [y, yr, y2, yl]
    ydev = [{"fsdp": z * NY + yy} for yy in ys]

    barrier = pltpu.get_barrier_semaphore()
    zpeers = [{"fsdp": (z + k) % NZ * NY + y} for k in range(1, NZ)]
    peers = [right, left, ydev[2], mate] + zpeers
    for peer in peers:
        pl.semaphore_signal(barrier, inc=1, device_id=peer, device_id_type=MESH)

    def cols(c):
        return pl.ds(pl.multiple_of(c * width, width), width)

    sources = ((w_hbm, wts), (t_hbm, tgt), (m_hbm, mom), (s_hbm, sec))
    sinks = ((nmo, nm_hbm), (avg, avg_hbm))

    def load(c, j):
        src, dst = sources[j]
        return pltpu.make_async_copy(src.at[:, cols(c)], dst.at[c], in_sem.at[c, j])

    def write(c, j):
        src, dst = sinks[j]
        return pltpu.make_async_copy(src.at[c], dst.at[:, cols(c)], out_sem.at[c, j])

    def load_h(q):
        some = pl.ds(q * block, block)
        return pltpu.make_async_copy(h_hbm.at[:, some], hid.at[:, some], in_sem.at[q, 4])

    write_h = pltpu.make_async_copy(hgr, hg_hbm, out_sem.at[0, 2])

    def remote(src, dst, c, j, dev, k=None):
        return pltpu.make_async_remote_copy(
            src_ref=src,
            dst_ref=dst,
            send_sem=send_sem.at[c, j],
            recv_sem=recv_sem.at[c, j if k is None else k],
            device_id=dev,
            device_id_type=MESH,
        )

    lo = pl.ds(0, NZ // 2)
    hi = pl.ds(NZ // 2, NZ // 2)

    def ry_one(c):
        return [
            remote(part.at[c, lo, y2, main], got1.at[c, 0], c, 0, right),
            remote(part.at[c, hi, y2, main], got1.at[c, 1], c, 1, left),
        ]

    def ry_two(c):
        return [
            remote(part.at[c, :, yr, main], got2.at[c, 0], c, 2, right),
            remote(part.at[c, :, yl, main], got2.at[c, 1], c, 3, left),
        ]

    def gy_one(c):
        own = err.at[c, :, y, main]
        return [remote(own, own, c, 4, right), remote(own, own, c, 5, left)]

    def gy_two(c):
        one = err.at[c, lo, yl, main]
        two = err.at[c, hi, yr, main]
        return [remote(one, one, c, 6, right), remote(two, two, c, 7, left)]

    def side_ry(c):
        return [
            remote(part.at[c, z, ys[k], side], got5.at[c, k - 1], c, 8 + k, ydev[k])
            for k in (2, 1, 3)
        ]

    def side_gy(c):
        own = err.at[c, z, y, side]
        return [remote(own, own, c, 11 + k, ydev[k]) for k in (2, 1, 3)]

    half = units // 2
    halves = [pl.ds(0, half), pl.ds(half, half)]

    def swap(c):
        return [
            remote(upd.at[c, part_rows], got6.at[c, part_rows], c, j, mate)
            for part_rows, j in zip(halves, (8, 31))
        ]

    sends = (ry_one, ry_two, gy_one, gy_two, swap, side_ry, side_gy)

    def start(copies):
        for copy in copies:
            copy.start()

    def arrived(copies):
        for copy in copies:
            copy.wait_recv()

    def zdev(zz):
        return {"fsdp": zz * NY + y}

    class Line:
        def __init__(self, view, got, fwd, base):
            self.view, self.got, self.fwd, self.base = view, got, fwd, base

        def move(self, src, dst, c, j, k, zz):
            return remote(src, dst, c, self.base + j, zdev(zz), self.base + k)

        def sum_end(self, c):
            two, one = self.view(part, c, beyond), self.view(part, c, near)
            return [
                self.move(two, self.fwd.at[c], c, 0, 0, near),
                self.move(one, self.got.at[c, 0], c, 1, 1, near),
            ]

        def sum_inner(self, c):
            one = self.view(part, c, outer)
            return [self.move(one, self.got.at[c, 0], c, 1, 1, outer)]

        def sum_on(self, c):
            one, two = self.view(part, c, far), self.view(part, c, twin)
            return [
                self.move(one, self.got.at[c, 1], c, 3, 2, far),
                self.move(two, self.got.at[c, 1], c, 2, 2, twin),
            ]

        def sum_start(self, c):
            @pl.when(end)
            def _():
                start(self.sum_end(c))

            @pl.when(inner)
            def _():
                start(self.sum_inner(c))

        def sum_forward(self, c):
            @pl.when(inner)
            def _():
                two = self.view(part, c, across)
                self.move(two, self.fwd.at[c], c, 0, 0, outer).wait_recv()
                two[...] = (f32(two[...]) + f32(self.fwd[c])).astype(BF16)
                start(self.sum_on(c))

        def sum_finish(self, c):
            own = self.view(part, c, z)
            for k in range(2):
                got = self.got.at[c, k]
                self.move(got, got, c, 1 + k, 1 + k, twin).wait_recv()
            return f32(own[...]) + f32(self.got[c, 0]) + f32(self.got[c, 1])

        def share_end(self, c):
            own = self.view(err, c, z)
            return [
                self.move(own, own, c, 4, 6, mid),
                self.move(own, own, c, 5, 4, near),
            ]

        def share_inner(self, c):
            own = self.view(err, c, z)
            return [
                self.move(own, own, c, 4, 5, twin),
                self.move(own, own, c, 5, 4, outer),
            ]

        def share_on(self, c):
            two = self.view(err, c, across)
            return [self.move(two, two, c, 6, 7, outer)]

        def share_start(self, c):
            @pl.when(end)
            def _():
                start(self.share_end(c))

            @pl.when(inner)
            def _():
                start(self.share_inner(c))

        def share_forward(self, c):
            own = self.view(err, c, z)
            self.move(own, own, c, 4, 4, twin).wait_recv()

            @pl.when(inner)
            def _():
                for k in (5, 6):
                    self.move(own, own, c, 4, k, twin).wait_recv()
                start(self.share_on(c))

        def share_finish(self, c):
            @pl.when(end)
            def _():
                two = self.view(err, c, beyond)
                self.move(two, two, c, 6, 7, twin).wait_recv()

        def sent(self, c):
            @pl.when(end)
            def _():
                for copy in self.sum_end(c) + self.share_end(c):
                    copy.wait_send()

            @pl.when(inner)
            def _():
                copies = self.sum_inner(c) + self.sum_on(c)
                for copy in copies + self.share_inner(c) + self.share_on(c):
                    copy.wait_send()

    def main_view(ref, c, zz):
        return ref.at[c, zz, y, main]

    def side_view(ref, c, zz):
        return ref.at[c, zz, :, side]

    main_line = Line(main_view, main_got, main_fwd, 15)
    side_line = Line(side_view, side_got, side_fwd, 23)

    load(0, 0).start()
    for q in range(NZ):
        load_h(q).start()

    @pl.loop(1, chunks)
    def _(c):
        load(c, 0).start()

    @pl.loop(0, chunks)
    def _(c):
        for j in range(1, 4):
            load(c, j).start()

    def stage0(c):
        load(c, 0).wait()

        @pl.when(c == 0)
        def _():
            for q in range(NZ):
                load_h(q).wait()
                hid_t[q] = hid[:, q * block : (q + 1) * block].T

        def terms(q):
            term = jnp.dot(hid_t[q], wts[c], preferred_element_type=F32)
            part[c, q] = term.astype(BF16).reshape(NY, rows, width)

        one, two = ry_one(c)
        pl.loop(0, NZ // 2)(terms)

        @pl.when(c == 0)
        def _():
            pl.semaphore_wait(barrier, len(peers))

        one.start()
        pl.loop(NZ // 2, NZ)(terms)
        two.start()
        side_line.sum_start(c)

    def stage1(c):
        arrived(ry_one(c))
        part[c, lo, yr, main] = (f32(part[c, lo, yr, main]) + f32(got1[c, 0])).astype(BF16)
        part[c, hi, yl, main] = (f32(part[c, hi, yl, main]) + f32(got1[c, 1])).astype(BF16)
        start(ry_two(c))
        side_line.sum_forward(c)

    def stage2(c):
        total = side_line.sum_finish(c)
        part[c, z, :, side] = total.astype(BF16)
        start(side_ry(c))
        arrived(ry_two(c))
        total = f32(part[c, :, y, main]) + f32(got2[c, 0]) + f32(got2[c, 1])
        part[c, :, y, main] = total.astype(BF16)
        main_line.sum_start(c)

    def stage3(c):
        load(c, 1).wait()
        arrived(side_ry(c))
        total = f32(part[c, z, y, side]) + f32(got5[c, 0])
        total += f32(got5[c, 1]) + f32(got5[c, 2])
        err[c, z, y, side] = (total - f32(tgt[c, side])).astype(BF16)
        start(side_gy(c))
        main_line.sum_forward(c)

    def stage4(c):
        arrived(side_gy(c))
        side_line.share_start(c)
        total = main_line.sum_finish(c)
        err[c, z, y, main] = (total - f32(tgt[c, main])).astype(BF16)
        main_line.share_start(c)

    def stage5(c):
        side_line.share_forward(c)
        main_line.share_forward(c)

    def stage6(c):
        main_line.share_finish(c)
        start(gy_one(c))

    def stage7(c):
        arrived(gy_one(c))
        start(gy_two(c))

    def stage8(c):
        side_line.share_finish(c)
        arrived(gy_two(c))
        load(c, 2).wait()
        load(c, 3).wait()
        gsum[...] = jnp.dot(
            hid[...], err[c].reshape(tokens, width), preferred_element_type=F32
        )
        for move, some in zip(swap(c), halves):
            grad = gsum[some] * (1.0 / tokens)
            weight = f32(wts[c, some])
            first = 0.9 * f32(mom[c, some]) + 0.1 * grad
            second = 0.95 * f32(sec[c, some]) + 0.05 * grad * grad
            step = (first * (1.0 / corr_first)) / (
                jnp.sqrt(second * (1.0 / corr_second)) + 1e-08
            )
            upd[c, some] = (weight - 0.02 * (step + 0.1 * weight)).astype(BF16)
            move.start()
            nmo[c, some] = first.astype(BF16)
        write(c, 0).start()

        @pl.when(c == 0)
        def _():
            acc[...] = jnp.zeros_like(acc)

        @pl.loop(0, NZ)
        def _(q):
            acc[q] += lax.dot_general(
                wts[c],
                err[c, q].reshape(block, width),
                (((1,), (1,)), ((), ())),
                preferred_element_type=F32,
            )

        @pl.when(c == last)
        def _():
            for q in range(NZ):
                hgr[:, q * block : (q + 1) * block] = acc[q].astype(BF16)
            write_h.start()

    def stage9(c):
        for move, some in zip(swap(c), halves):
            move.wait_recv()
            both = f32(upd[c, some]) + f32(got6[c, some])
            avg[c, some] = (both * 0.5).astype(BF16)
        write(c, 1).start()
        main_line.sent(c)
        side_line.sent(c)
        for copies in sends:
            for copy in copies(c):
                copy.wait_send()

    stages = (
        (0, stage0),
        (1, stage1),
        (2, stage2),
        (3, stage3),
        (4, stage4),
        (5, stage5),
        (6, stage6),
        (7, stage7),
        (8, stage8),
        (9, stage9),
    )

    @pl.loop(0, chunks + 9)
    def _(t):
        for lag, stage in stages:
            c = t - lag

            @pl.when((c >= 0) & (c < chunks))
            def _(c=c, stage=stage):
                stage(c)

    write_h.wait()

    @pl.loop(0, chunks)
    def _(c):
        for j in range(2):
            write(c, j).wait()


def round_at(level, hidden, target, weights, moment, second):
    units, model = weights.shape
    tokens = hidden.shape[1]
    rows = target.shape[0]
    width = min(WIDTH, model)
    chunks = model // width
    block = NY * rows
    whole = jax.ShapeDtypeStruct((units, model), BF16)
    per_chunk = (chunks, units, width)
    return pl.pallas_call(
        functools.partial(kernel, level),
        out_shape=(whole, whole, jax.ShapeDtypeStruct((units, tokens), BF16)),
        in_specs=[pl.BlockSpec(memory_space=pl.ANY)] * 5,
        out_specs=[pl.BlockSpec(memory_space=pl.ANY)] * 3,
        scratch_shapes=[
            pltpu.VMEM((units, tokens), BF16),
            pltpu.VMEM((NZ, block, units), BF16),
            pltpu.VMEM(per_chunk, BF16),
            pltpu.VMEM(per_chunk, BF16),
            pltpu.VMEM(per_chunk, BF16),
            pltpu.VMEM((chunks, rows, width), BF16),
            pltpu.VMEM((chunks, NZ, NY, rows, width), BF16),
            pltpu.VMEM((chunks, 2, NZ // 2, rows - SIDE, width), BF16),
            pltpu.VMEM((chunks, 2, NZ, rows - SIDE, width), BF16),
            pltpu.VMEM((chunks, 2, rows - SIDE, width), BF16),
            pltpu.VMEM((chunks, 2, rows - SIDE, width), BF16),
            pltpu.VMEM((chunks, 2, NY, SIDE, width), BF16),
            pltpu.VMEM((chunks, 2, NY, SIDE, width), BF16),
            pltpu.VMEM((chunks, NY - 1, SIDE, width), BF16),
            pltpu.VMEM((chunks, NZ, NY, rows, width), BF16),
            pltpu.VMEM((NZ, units, block), F32),
            pltpu.VMEM((units, width), F32),
            pltpu.VMEM(per_chunk, BF16),
            pltpu.VMEM(per_chunk, BF16),
            pltpu.VMEM(per_chunk, BF16),
            pltpu.VMEM(per_chunk, BF16),
            pltpu.VMEM((units, tokens), BF16),
            pltpu.SemaphoreType.DMA((max(chunks, NZ), 5)),
            pltpu.SemaphoreType.DMA((chunks, 3)),
            pltpu.SemaphoreType.DMA((chunks, 32)),
            pltpu.SemaphoreType.DMA((chunks, 32)),
        ],
        compiler_params=pltpu.CompilerParams(
            collective_id=level,
            has_side_effects=True,
            vmem_limit_bytes=50 * 1024 * 1024,
        ),
    )(hidden, target, weights, moment, second)


def local(hidden, target, weights, moment, second, round_index):
    levels = 1
    while levels < LEVELS and 2 << levels <= lax.axis_size("rep"):
        levels += 1
    branches = [functools.partial(round_at, level) for level in range(levels)]
    chosen = jnp.remainder(round_index[0], levels)
    averaged, new_moment, hidden_grad = lax.switch(
        chosen, branches, hidden[0], target[0], weights[0], moment[0], second[0]
    )
    return (averaged[None], new_moment[None], hidden_grad[None])


def solution(mesh):
    split = P("rep", "fsdp", None)
    return jax.shard_map(
        local,
        mesh=mesh,
        in_specs=(split,) * 5 + (P(),),
        out_specs=(split,) * 3,
        check_vma=False,
    )
```
